512 devices in a mesh: ctx: 64 (over x, y_lo, z), head: 8 (over y_hi, core).
Axes of the slice: x: 4, y: 8 (y_hi: 4, y_lo: 2; y = y_hi * 2 + y_lo), z: 8, core: 2. Of those that a mesh axis runs over, the one named last changes fastest.
Arguments:
- queries: bfloat16 [16384, 8192], P(('ctx', 'head')), may hold values from -6 to 6
- grad_out: bfloat16 [16384, 8192], P(('ctx', 'head')), may hold values from -3 to 3
- outputs: bfloat16 [16384, 8192], P(('ctx', 'head')), may hold values from -3 to 3
- keys: bfloat16 [16384, 1024], P(('ctx', 'head')), may hold values from -6 to 6
- values: bfloat16 [16384, 1024], P(('ctx', 'head')), may hold values from -6 to 6
- log_sum_exp: float32 [16384, 64], P(('ctx', 'head')), may hold values from 1 to 4
- doc_start: int32 [16384], P('ctx'), may hold values from 0 to 16383, as said below
Outputs:
- grad_queries: bfloat16 [16384, 8192], P(('ctx', 'head'))
- grad_keys: float32 [16384, 1024], P('ctx', 'head')
- grad_values: float32 [16384, 1024], P('ctx', 'head')
The draws below stay inside these ranges and needn't reach their ends.
Inputs may be any that keep to these rules, and one draw needn't show every extreme that they name: doc_start never falls along the sequence, doc_start[t] <= t, and doc_start[t] is the position where a document begins (doc_start[doc_start[t]] = doc_start[t]); every document holds at most 1536 tokens and some document holds exactly 1536.
All inputs are finite; a program needn't handle non-finite values.
Results may differ from the reference program's by a relative error of at most 0.0061.
Values may be sent and summed in bfloat16 or wider, within the bound.
No kernel may reach another device: no remote copies, remote signals or barrier semaphores. Data moves between devices by JAX's collectives and lax.ppermute only.
A program may use at most 64 MiB of HBM per device.

```python
import jax
import jax.numpy as jnp
from jax import lax

QH = 64
KVH = 8
HD = 128
TOK_DEV = 256
REACH = 6
MAXDOC = 1536
TOKENS = 16384


def draw_doc_start(key, part):
    key = jax.random.fold_in(key, 11)
    key_off, key_clean, key_level, key_bits = jax.random.split(key, 4)
    pos = jnp.arange(TOKENS, dtype=jnp.int32)
    offset = jax.random.randint(key_off, (), 1, TOK_DEV, dtype=jnp.int32)
    windows = (TOKENS - offset) // MAXDOC
    clean = jax.random.randint(key_clean, (), 0, 1 << 20, dtype=jnp.int32) % windows
    forced = pos % MAXDOC == offset
    level = jax.random.randint(key_level, (TOKENS // TOK_DEV,), 0, 3, dtype=jnp.int32)
    limits = jnp.array([8, 1, 0], jnp.int32)[level]
    limit_tok = jnp.repeat(limits, TOK_DEV)
    extra = jax.random.randint(key_bits, (TOKENS,), 0, 64, dtype=jnp.int32) < limit_tok
    lower = offset + clean * MAXDOC
    inside = (pos > lower) & (pos < lower + MAXDOC)
    bound = forced | extra & jnp.logical_not(inside) | (pos == 0)
    return lax.cummax(jnp.where(bound, pos, 0), axis=0).astype(jnp.int32)


def level_of(stream_key, dims, pieces, least, largest):
    level, own = 1.0, jax.random.fold_in(stream_key, 6)
    for position, shards_of in pieces:
        steps = jnp.exp(jax.random.uniform(jax.random.fold_in(own, position), (shards_of,), jnp.float32, least / len(pieces), largest / len(pieces)))
        level = level * jnp.repeat(steps, dims[position] // shards_of).reshape([-1 if axis == position else 1 for axis in range(len(dims))])
    return level


def normal_values(stream_key, dims, deviation, limit, cuts=(), kind=jnp.bfloat16):
    gain = level_of(stream_key, dims, cuts, -0.22, 0.18) if cuts else 1.0
    drawn = jax.random.normal(stream_key, dims, jnp.float32) * deviation * gain
    return jnp.minimum(jnp.maximum(drawn, -limit), limit).astype(kind)


def setup_inputs(seed: int = 0) -> dict:
    seeds = jax.random.split(jax.random.key(seed), 8)
    queries = normal_values(seeds[0], (TOKENS, QH * HD), 1.0, 6.0, ((0, 512),))
    grad_out = normal_values(seeds[1], (TOKENS, QH * HD), 0.5, 3.0, ((0, 512),))
    outputs = normal_values(seeds[2], (TOKENS, QH * HD), 0.5, 3.0, ((0, 512),))
    keys = normal_values(seeds[3], (TOKENS, KVH * HD), 1.0, 6.0, ((0, 512),))
    values = normal_values(seeds[4], (TOKENS, KVH * HD), 1.0, 6.0, ((0, 512),))
    log_sum_exp = jnp.clip(1.0 + 3.0 * jax.random.uniform(seeds[5], (TOKENS, QH), jnp.float32) ** level_of(seeds[5], (TOKENS, QH), ((0, 512),), -0.2, 0.2), 1.0, 4.0)
    doc_start = draw_doc_start(jax.random.fold_in(seeds[7], 71), 0)
    return dict(queries=queries, grad_out=grad_out, outputs=outputs, keys=keys, values=values, log_sum_exp=log_sum_exp, doc_start=doc_start)


def reference(queries, grad_out, outputs, keys, values, log_sum_exp, doc_start):
    group = QH // KVH
    scale = HD ** -0.5
    width = (REACH + 1) * TOK_DEV
    front = REACH * TOK_DEV
    delta = jnp.sum((grad_out.astype(jnp.float32) * outputs.astype(jnp.float32)).reshape(TOKENS, QH, HD), axis=2)
    key_pad = jnp.concatenate([jnp.zeros((front, KVH * HD), jnp.bfloat16), keys], axis=0)
    value_pad = jnp.concatenate([jnp.zeros((front, KVH * HD), jnp.bfloat16), values], axis=0)

    def step(carry, index):
        grad_k, grad_v = carry
        row0 = (index * TOK_DEV).astype(jnp.int32)
        query = lax.dynamic_slice_in_dim(queries, row0, TOK_DEV, 0).reshape(TOK_DEV, KVH, group, HD).astype(jnp.float32)
        dout = lax.dynamic_slice_in_dim(grad_out, row0, TOK_DEV, 0).reshape(TOK_DEV, KVH, group, HD).astype(jnp.float32)
        lse = lax.dynamic_slice_in_dim(log_sum_exp, row0, TOK_DEV, 0).reshape(TOK_DEV, KVH, group)
        dlt = lax.dynamic_slice_in_dim(delta, row0, TOK_DEV, 0).reshape(TOK_DEV, KVH, group)
        start = lax.dynamic_slice_in_dim(doc_start, row0, TOK_DEV, 0)
        key = lax.dynamic_slice_in_dim(key_pad, row0, width, 0).reshape(width, KVH, HD).astype(jnp.float32)
        value = lax.dynamic_slice_in_dim(value_pad, row0, width, 0).reshape(width, KVH, HD).astype(jnp.float32)
        qpos = row0 + jnp.arange(TOK_DEV, dtype=jnp.int32)
        kpos = row0 - front + jnp.arange(width, dtype=jnp.int32)
        allowed = (kpos[None, :] >= start[:, None]) & (kpos[None, :] <= qpos[:, None])
        score = jnp.einsum('tghd,wgd->tghw', query, key) * scale
        prob = jnp.where(allowed[:, None, None, :], jnp.exp(score - lse[..., None]), 0.0)
        grad_prob = jnp.einsum('tghd,wgd->tghw', dout, value)
        grad_score = prob * (grad_prob - dlt[..., None])
        prob_half = lax.optimization_barrier(prob.astype(jnp.bfloat16)).astype(jnp.float32)
        score_half = lax.optimization_barrier(grad_score.astype(jnp.bfloat16)).astype(jnp.float32)
        grad_q = (jnp.einsum('tghw,wgd->tghd', score_half, key) * scale).astype(jnp.bfloat16)
        part_k = jnp.einsum('tghw,tghd->wgd', score_half, query) * scale
        part_v = jnp.einsum('tghw,tghd->wgd', prob_half, dout)
        old_k = lax.dynamic_slice_in_dim(grad_k, row0, width, 0)
        old_v = lax.dynamic_slice_in_dim(grad_v, row0, width, 0)
        grad_k = lax.dynamic_update_slice_in_dim(grad_k, old_k + part_k.reshape(width, KVH * HD), row0, 0)
        grad_v = lax.dynamic_update_slice_in_dim(grad_v, old_v + part_v.reshape(width, KVH * HD), row0, 0)
        return (grad_k, grad_v), grad_q.reshape(TOK_DEV, QH * HD)

    zeros = jnp.zeros((front + TOKENS, KVH * HD), jnp.float32)
    (grad_k, grad_v), grad_q = lax.scan(step, (zeros, zeros), jnp.arange(TOKENS // TOK_DEV, dtype=jnp.int32))
    return grad_q.reshape(TOKENS, QH * HD), grad_k[front:], grad_v[front:]
```

```python
import functools
import math

import jax
import jax.numpy as jnp
from jax import lax
from jax.experimental import pallas as pl
from jax.experimental.pallas import tpu as pltpu
from jax.sharding import PartitionSpec as P

REACH = 6
HD = 128
AUX = 16
LOG2E = math.log2(math.e)
F32 = jnp.float32
BF16 = jnp.bfloat16
VMEM_LIMIT = 32 * 1024 * 1024
VMEM = pl.BlockSpec(memory_space=pltpu.VMEM)
LAST = (((1,), (1,)), ((), ()))
FIRST = (((0,), (0,)), ((), ()))


def call(kernel, outs, scratch=(), flops=0, moved=0):
    return pl.pallas_call(
        kernel,
        out_shape=outs,
        scratch_shapes=scratch,
        compiler_params=pltpu.CompilerParams(vmem_limit_bytes=VMEM_LIMIT),
        cost_estimate=pl.CostEstimate(flops=flops, bytes_accessed=moved, transcendentals=0),
    )


def pack_keys(groups, key_ref, value_ref, out_ref):
    rows = key_ref.shape[0]
    for g in range(groups):
        out_ref[g, :rows, :] = key_ref[:, g * HD : (g + 1) * HD]
        out_ref[g, rows:, :] = value_ref[:, g * HD : (g + 1) * HD]


def three_parts(x):
    first = x.astype(BF16)
    rest = x - first.astype(F32)
    second = rest.astype(BF16)
    third = (rest - second.astype(F32)).astype(BF16)
    return first, second, third


def lane_sums(x):
    ones = jnp.ones((8, HD), BF16)
    return sum(lax.dot_general(ones, part, LAST, preferred_element_type=F32) for part in three_parts(x))


def pack_queries(groups, per, query_ref, dout_ref, output_ref, lse_ref, out_ref):
    rows = query_ref.shape[0]
    span = per * rows
    lse = jnp.concatenate([lse_ref[...] * LOG2E, jnp.zeros((rows, HD - groups * per), F32)], axis=1)
    lane = lax.broadcasted_iota(jnp.int32, (rows, HD), 1)
    for g in range(groups):
        products, picked = [], []
        for h in range(per):
            cols = slice((g * per + h) * HD, (g * per + h + 1) * HD)
            dout = dout_ref[:, cols]
            out_ref[g, h * rows : (h + 1) * rows, :] = query_ref[:, cols]
            out_ref[g, span + h * rows : span + (h + 1) * rows, :] = dout
            products.append(dout.astype(F32) * output_ref[:, cols].astype(F32))
            picked.append(jnp.where(lane == g * per + h, lse, 0.0))
        pieces = []
        for sums in (lane_sums(jnp.concatenate(picked, 0)), lane_sums(jnp.concatenate(products, 0))):
            line = sums[:1]
            high = line.astype(BF16).astype(F32)
            for part in (high, line - high):
                pieces += [part[:, k * HD : (k + 1) * HD] for k in range(span // HD)]
        pieces.append(jnp.zeros((AUX - len(pieces), HD), F32))
        out_ref[g, 2 * span :, :] = jnp.concatenate(pieces, 0).astype(BF16)


def attention(scale, chunks, rows, per, low_ref, pos_ref, msg_ref, *refs):
    kv_refs = refs[: REACH + 1]
    dq_ref, own_ref, p1, p2, p3, p4, p5, p6, kv_all, part_all, prob_ref, ds_ref, dqt_ref = refs[REACH + 1 :]
    span = per * rows
    block = chunks * rows
    for s in range(REACH + 1):
        kv_all[s] = kv_refs[s][...]
    dqt_ref[...] = jnp.zeros_like(dqt_ref)
    kappa = lax.broadcasted_iota(jnp.int32, (block, span), 0)

    def one_block(s, diagonal):
        kv = kv_all[s].reshape(chunks, 2, rows, HD)
        key = kv[:, 0].reshape(block, HD)
        value = kv[:, 1].reshape(block, HD)
        key_t = key.T
        kpos = kappa - s * block
        for j in range(chunks):
            cols = slice(j * span, (j + 1) * span)
            query = msg_ref[j, :span, :]
            dout = msg_ref[j, span : 2 * span, :]
            aux = msg_ref[j, 2 * span :, :].astype(F32)
            half = span // HD

            def line(at):
                return jnp.concatenate([aux[at + k : at + k + 1] + aux[at + half + k : at + half + k + 1] for k in range(half)], 1)

            lse, delta = line(0), line(2 * half)
            score = lax.dot_general(key, query, LAST, preferred_element_type=F32)
            allowed = kpos >= low_ref[j : j + 1, :]
            if diagonal:
                allowed = allowed & (kpos <= pos_ref[j : j + 1, :])
            prob = jnp.where(allowed, jnp.exp2(score * (scale * LOG2E) - lse), 0.0)
            grad_prob = lax.dot_general(value, dout, LAST, preferred_element_type=F32)
            ds = (prob * (grad_prob - delta)).astype(BF16)
            prob_ref[:, cols] = prob.astype(BF16)
            ds_ref[:, cols] = ds
            dqt_ref[:, cols] += jnp.dot(key_t, ds, preferred_element_type=F32)
        queries = jnp.concatenate([msg_ref[j, :span, :] for j in range(chunks)], 0)
        douts = jnp.concatenate([msg_ref[j, span : 2 * span, :] for j in range(chunks)], 0)
        part_all[s, :block] = jnp.dot(ds_ref[...], queries, preferred_element_type=F32) * scale
        part_all[s, block:] = jnp.dot(prob_ref[...], douts, preferred_element_type=F32)

    one_block(0, True)

    def step(s, carry):
        one_block(s, False)
        return carry

    lax.fori_loop(1, REACH + 1, step, 0)
    own_ref[...] = part_all[0]
    for s, ref in enumerate((p1, p2, p3, p4, p5, p6), 1):
        ref[...] = part_all[s].astype(ref.dtype)
    for j in range(chunks):
        dq_ref[j] = (dqt_ref[:, j * span : (j + 1) * span] * scale).T.astype(BF16)


def unpack(groups, per, got_ref, out_ref):
    rows = out_ref.shape[0]
    for g in range(groups):
        for h in range(per):
            out_ref[:, (g * per + h) * HD : (g * per + h + 1) * HD] = got_ref[g, h * rows : (h + 1) * rows, :]


def shift(array, by):
    size = lax.axis_size("ctx")
    return lax.ppermute(array, "ctx", [(i, (i + by) % size) for i in range(size)])


def exchange(array):
    groups, rows, cols = array.shape
    flat = array.reshape(groups * rows, cols)
    return lax.all_to_all(flat, "head", split_axis=0, concat_axis=0, tiled=True).reshape(array.shape)


def per_device(queries, grad_out, outputs, keys, values, log_sum_exp, doc_start):
    rows, wide = queries.shape
    heads = log_sum_exp.shape[1]
    groups = keys.shape[1] // HD
    per = heads // groups
    span = per * rows
    block = doc_start.shape[0]
    chunks = block // rows
    scale = HD ** (-0.5)
    shape = jax.ShapeDtypeStruct

    kv_message = call(
        functools.partial(pack_keys, groups), shape((groups, 2 * rows, HD), BF16), moved=4 * rows * groups * HD * 2
    )(keys, values)
    kv_own = exchange(kv_message)
    message = call(
        functools.partial(pack_queries, groups, per),
        shape((groups, 2 * span + AUX, HD), BF16),
        moved=5 * rows * wide * 2,
    )(queries, grad_out, outputs, log_sum_exp)
    message, kv_own = lax.optimization_barrier((message, kv_own))
    kv = [kv_own.reshape(2 * block, HD)]
    got = exchange(message)

    kv1 = shift(kv[0], 1)
    kv6 = shift(kv[0], 6)
    kv2 = shift(kv1, 1)
    kv5 = shift(kv6, -1)
    kv3 = shift(kv2, 1)
    kv4 = shift(kv5, -1)

    first = lax.axis_index("ctx") * block
    low = jnp.tile((doc_start - first).reshape(chunks, 1, rows), (1, per, 1)).reshape(chunks, span)
    pos = jnp.tile(jnp.arange(block, dtype=jnp.int32).reshape(chunks, 1, rows), (1, per, 1)).reshape(chunks, span)

    part32, part16 = shape((2 * block, HD), F32), shape((2 * block, HD), BF16)
    dq, own, g1, g2, g3, g4, g5, g6 = call(
        functools.partial(attention, scale, chunks, rows, per),
        [shape((chunks, span, HD), BF16), part32, part32, part32, part16, part16, part32, part32],
        scratch=[
            pltpu.VMEM((REACH + 1, 2 * block, HD), BF16),
            pltpu.VMEM((REACH + 1, 2 * block, HD), F32),
            pltpu.VMEM((block, chunks * span), BF16),
            pltpu.VMEM((block, chunks * span), BF16),
            pltpu.VMEM((HD, chunks * span), F32),
        ],
        flops=10 * (REACH + 1) * block * chunks * span * HD,
        moved=6 * 1024 * 1024,
    )(low, pos, got, kv[0], kv1, kv2, kv3, kv4, kv5, kv6)

    back_q = exchange(dq)
    near = shift(g3, -1)
    far = shift(g4, 1)
    near = shift((g2 + near.astype(F32)).astype(BF16), -1)
    far = shift((g5 + far.astype(F32)).astype(BF16), 1)
    near = shift((g1 + near.astype(F32)).astype(BF16), -1)
    far = shift((g6 + far.astype(F32)).astype(BF16), -6)
    total = own + near.astype(F32) + far.astype(F32)

    grad_q = call(functools.partial(unpack, groups, per), shape((rows, wide), BF16), moved=4 * rows * wide)(back_q)
    return grad_q, total[:block], total[block:]


def solution(mesh):
    split = P(("ctx", "head"), None)
    return jax.shard_map(
        per_device,
        mesh=mesh,
        in_specs=(split, split, split, split, split, split, P("ctx")),
        out_specs=(split, P("ctx", "head"), P("ctx", "head")),
        check_vma=False,
    )
```

```python
import functools
import math

import jax
import jax.numpy as jnp
from jax import lax
from jax.experimental import pallas as pl
from jax.experimental.pallas import tpu as pltpu
from jax.sharding import Mesh
from jax.sharding import PartitionSpec as P

REACH = 6
HD = 128
RING = 8
AUX = 16
LOG2E = math.log2(math.e)
F32 = jnp.float32
BF16 = jnp.bfloat16
VMEM_LIMIT = 32 * 1024 * 1024
PACK_LIMIT = 60 * 1024 * 1024
LAST = (((1,), (1,)), ((), ()))


def call(kernel, outs, scratch=(), flops=0, moved=0, limit=VMEM_LIMIT, **specs):
    return pl.pallas_call(
        kernel,
        out_shape=outs,
        scratch_shapes=scratch,
        compiler_params=pltpu.CompilerParams(vmem_limit_bytes=limit),
        cost_estimate=pl.CostEstimate(flops=flops, bytes_accessed=moved, transcendentals=0),
        **specs,
    )


def pack_keys(groups, key_ref, value_ref, out_ref, sems):
    rows = key_ref.shape[0]
    copies = []
    for g in range(groups):
        for k, ref in enumerate((key_ref, value_ref)):
            copy = pltpu.make_async_copy(
                ref.at[:, g * HD : (g + 1) * HD], out_ref.at[g, k * rows : (k + 1) * rows, :], sems.at[g, k]
            )
            copy.start()
            copies.append(copy)
    for copy in copies:
        copy.wait()


def three_parts(x):
    first = x.astype(BF16)
    rest = x - first.astype(F32)
    second = rest.astype(BF16)
    third = (rest - second.astype(F32)).astype(BF16)
    return first, second, third


def lane_sums(x):
    ones = jnp.ones((8, HD), BF16)
    return sum(lax.dot_general(ones, part, LAST, preferred_element_type=F32) for part in three_parts(x))


def fetch(pairs, sems):
    copies = []
    for n, (source, target) in enumerate(pairs):
        half = source.shape[0] // 2
        for k in range(2):
            rows = slice(k * half, (k + 1) * half)
            copies.append(pltpu.make_async_copy(source.at[rows], target.at[rows], sems.at[n, k]))
    for copy in copies:
        copy.start()
    for copy in copies:
        copy.wait()


def pack_queries(groups, per, query_hbm, dout_hbm, output_hbm, lse_hbm, out_ref, q_ref, d_ref, o_ref, l_ref, sems):
    rows = q_ref.shape[0]
    span = per * rows
    fetch(((query_hbm, q_ref), (dout_hbm, d_ref), (output_hbm, o_ref), (lse_hbm, l_ref)), sems)
    lse = jnp.concatenate([l_ref[...] * LOG2E, jnp.zeros((rows, HD - groups * per), F32)], axis=1)
    lane = lax.broadcasted_iota(jnp.int32, (rows, HD), 1)
    for g in range(groups):
        products, picked = [], []
        for h in range(per):
            cols = slice((g * per + h) * HD, (g * per + h + 1) * HD)
            dout = d_ref[:, cols]
            out_ref[g, h * rows : (h + 1) * rows, :] = q_ref[:, cols]
            out_ref[g, span + h * rows : span + (h + 1) * rows, :] = dout
            products.append(dout.astype(F32) * o_ref[:, cols].astype(F32))
            picked.append(jnp.where(lane == g * per + h, lse, 0.0))
        pieces = []
        for sums in (lane_sums(jnp.concatenate(picked, 0)), lane_sums(jnp.concatenate(products, 0))):
            line = sums[:1]
            high = line.astype(BF16).astype(F32)
            for part in (high, line - high):
                pieces += [part[:, k * HD : (k + 1) * HD] for k in range(span // HD)]
        pieces.append(jnp.zeros((AUX - len(pieces), HD), F32))
        out_ref[g, 2 * span :, :] = jnp.concatenate(pieces, 0).astype(BF16)


def attention(scale, chunks, rows, per, blocks, sources, sinks, first, last, low_ref, pos_ref, msg_ref, *refs):
    count = len(blocks)
    operands = 1 + max(n for n, _ in sources)
    kv_refs, refs = refs[:operands], refs[operands:]
    if not first:
        before_ref, refs = refs[0], refs[1:]
    dq_ref, part_refs, refs = refs[0], refs[1 : len(sinks) + 1], refs[len(sinks) + 1 :]
    k_all, v_all, kt_all, dk_ref, dv_ref = refs[:5]
    bufs = (refs[5:9], refs[9:13])
    span = per * rows
    block = chunks * rows
    half = span // HD
    total = count * block
    for n, (operand, slot) in enumerate(sources):
        at = slice(n * block, (n + 1) * block)
        kv = kv_refs[operand][slot * 2 * block : (slot + 1) * 2 * block].reshape(chunks, 2, rows, HD)
        key = kv[:, 0].reshape(block, HD)
        k_all[at] = key
        v_all[at] = kv[:, 1].reshape(block, HD)
        kt_all[:, at] = key.T
    dk_ref[...] = jnp.zeros_like(dk_ref)
    dv_ref[...] = jnp.zeros_like(dv_ref)

    def window_of(j):
        begin = j * rows if blocks[0] == REACH else 0
        end = total - block + (j + 1) * rows if blocks[-1] == 0 else total
        return begin, end

    def scores(j, sc, gp):
        begin, end = window_of(j)
        sc[: end - begin] = lax.dot_general(k_all[begin:end], msg_ref[j, :span, :], LAST, preferred_element_type=F32)
        gp[: end - begin] = lax.dot_general(
            v_all[begin:end], msg_ref[j, span : 2 * span, :], LAST, preferred_element_type=F32
        )

    def middle(j, sc, gp, pb, ds):
        aux = msg_ref[j, 2 * span :, :].astype(F32)

        def line(at):
            return jnp.concatenate([aux[at + k : at + k + 1] + aux[at + half + k : at + half + k + 1] for k in range(half)], 1)

        lse, delta = line(0), line(2 * half)
        low, pos = low_ref[j : j + 1, :], pos_ref[j : j + 1, :]
        begin, end = window_of(j)
        old_begin, old_end = window_of(j - 2) if j >= 2 else (0, total)
        for a, b in ((old_begin, begin), (end, old_end)):
            if a < b:
                ds[a:b] = jnp.zeros((b - a, span), BF16)
        for n in range(count):
            start, stop = max(begin, n * block), min(end, (n + 1) * block)
            if start >= stop:
                continue
            size = stop - start
            at = slice(start - begin, stop - begin)
            kpos = lax.broadcasted_iota(jnp.int32, (size, span), 0) + (start - n * block - blocks[n] * block)
            allowed = kpos >= low
            if blocks[n] == 0:
                allowed = allowed & (kpos <= pos)
            prob = jnp.where(allowed, jnp.exp2(sc[at] * (scale * LOG2E) - lse), 0.0)
            pb[at] = prob.astype(BF16)
            ds[start:stop] = (prob * (gp[at] - delta)).astype(BF16)

    def sums(j, pb, ds):
        begin, end = window_of(j)
        dv_ref[begin:end] += jnp.dot(pb[: end - begin], msg_ref[j, span : 2 * span, :], preferred_element_type=F32)
        dk_ref[begin:end] += jnp.dot(ds[begin:end], msg_ref[j, :span, :], preferred_element_type=F32)
        dqt = jnp.dot(kt_all[...], ds[...], preferred_element_type=F32)
        cols = slice(j * span, (j + 1) * span)
        if not first:
            dqt = dqt + before_ref[:, cols]
        if last:
            dq_ref[j] = (dqt * scale).T.astype(BF16)
        else:
            dq_ref[:, cols] = dqt

    scores(0, *bufs[0][:2])
    for j in range(chunks):
        sc, gp, pb, ds = bufs[j % 2]
        if j + 1 < chunks:
            scores(j + 1, *bufs[(j + 1) % 2][:2])
        middle(j, sc, gp, pb, ds)
        sums(j, pb, ds)
    for ref, held in zip(part_refs, sinks):
        for slot, s in enumerate(held):
            n = blocks.index(s)
            at = slice(n * block, (n + 1) * block)
            row = slot * 2 * block
            ref[row : row + block] = (dk_ref[at] * scale).astype(ref.dtype)
            ref[row + block : row + 2 * block] = dv_ref[at].astype(ref.dtype)


def attend(scale, chunks, rows, per, low, pos, got, blocks, kv, sources, sinks, before=None, last=False):
    shape = jax.ShapeDtypeStruct
    vmem = pl.BlockSpec(memory_space=pltpu.VMEM)
    span, block = per * rows, chunks * rows
    total = len(blocks) * block
    buffers = [
        pltpu.VMEM((total, span), F32),
        pltpu.VMEM((total, span), F32),
        pltpu.VMEM((total, span), BF16),
        pltpu.VMEM((total, span), BF16),
    ]
    dq = shape((chunks, span, HD), BF16) if last else shape((HD, chunks * span), F32)
    operands = [low, pos, got, *kv] + ([] if before is None else [before])
    return call(
        functools.partial(
            attention, scale, chunks, rows, per, blocks, sources, [held for _, held in sinks], before is None, last
        ),
        [dq] + [shape((len(held) * 2 * block, HD), kind) for kind, held in sinks],
        scratch=[
            pltpu.VMEM((total, HD), BF16),
            pltpu.VMEM((total, HD), BF16),
            pltpu.VMEM((HD, total), BF16),
            pltpu.VMEM((total, HD), F32),
            pltpu.VMEM((total, HD), F32),
            *buffers,
            *buffers,
        ],
        flops=10 * total * chunks * span * HD,
        moved=4 * 1024 * 1024,
        in_specs=[vmem] * len(operands),
        out_specs=[vmem] * (1 + len(sinks)),
    )(*operands)


def unpack(groups, per, got_ref, out_ref):
    rows = out_ref.shape[0]
    for g in range(groups):
        for h in range(per):
            out_ref[:, (g * per + h) * HD : (g * per + h + 1) * HD] = got_ref[g, h * rows : (h + 1) * rows, :]


def turn(array, axis, by):
    size = lax.axis_size(axis)
    return lax.ppermute(array, axis, [(i, (i + by) % size) for i in range(size)])


def hop(array, by):
    axes = ("ring", "z")
    size = lax.axis_size(axes)
    return lax.ppermute(array, axes, [(i, (i + by) % size) for i in range(size)])


def exchange(array):
    groups, rows, cols = array.shape
    flat = array.reshape(groups * rows, cols)
    return lax.all_to_all(flat, "head", split_axis=0, concat_axis=0, tiled=True).reshape(array.shape)


def per_device(queries, grad_out, outputs, keys, values, log_sum_exp, doc_start):
    rows, wide = queries.shape
    heads = log_sum_exp.shape[1]
    groups = keys.shape[1] // HD
    per = heads // groups
    span = per * rows
    block = doc_start.shape[0]
    chunks = block // rows
    scale = HD ** (-0.5)
    shape = jax.ShapeDtypeStruct
    hbm = pl.BlockSpec(memory_space=pltpu.HBM)
    vmem = pl.BlockSpec(memory_space=pltpu.VMEM)

    kv_own = call(
        functools.partial(pack_keys, groups),
        shape((groups, 2 * rows, HD), BF16),
        scratch=[pltpu.SemaphoreType.DMA((groups, 2))],
        moved=4 * rows * groups * HD * 2,
        in_specs=[hbm] * 2,
        out_specs=vmem,
        limit=PACK_LIMIT,
    )(keys, values)
    kv_own = exchange(kv_own)
    message = call(
        functools.partial(pack_queries, groups, per),
        shape((groups, 2 * span + AUX, HD), BF16),
        scratch=[pltpu.VMEM((rows, wide), BF16)] * 3
        + [pltpu.VMEM((rows, heads), F32), pltpu.SemaphoreType.DMA((4, 2))],
        moved=5 * rows * wide * 2,
        in_specs=[hbm] * 4,
        out_specs=vmem,
        limit=PACK_LIMIT,
    )(queries, grad_out, outputs, log_sum_exp)
    message, kv_own = lax.optimization_barrier((message, kv_own))
    kv_own = kv_own.reshape(2 * block, HD)
    kv_older = turn(kv_own, "ring", 1)
    message, kv_older = lax.optimization_barrier((message, kv_older))
    got = exchange(message)
    z = lax.axis_index("z")

    def behind(s):
        return turn(jnp.where(z + s < RING, kv_own, kv_older), "z", s)

    kv = {0: kv_own}
    for s in (3, 4, 5, 2, 6, 1):
        kv[s] = behind(s)

    first = (lax.axis_index("ring") * RING + z) * block
    low = jnp.tile((doc_start - first).reshape(chunks, 1, rows), (1, per, 1)).reshape(chunks, span)
    pos = jnp.tile(jnp.arange(block, dtype=jnp.int32).reshape(chunks, 1, rows), (1, per, 1)).reshape(chunks, span)

    run = functools.partial(attend, scale, chunks, rows, per, low, pos, got)

    dq, g14, g25 = run(
        (5, 4, 2, 1), [kv[s] for s in (5, 4, 2, 1)], [(n, 0) for n in range(4)], [(BF16, (1, 4)), (BF16, (2, 5))]
    )
    from_next = hop(g14, -1).astype(F32)
    from_last = hop(g25, 1).astype(F32)
    dq, g6, g3, g0 = run(
        (6, 3, 0),
        [kv[s] for s in (6, 3, 0)],
        [(n, 0) for n in range(3)],
        [(F32, (6,)), (F32, (3,)), (F32, (0,))],
        before=dq,
        last=True,
    )
    back_q = exchange(dq)
    size = 2 * block
    g3 = hop((g3 + from_next[size:] + from_last[:size]).astype(BF16), -3)
    g6 = hop((g6 + from_last[size:]).astype(BF16), -6)
    total = g0 + from_next[:size] + g3.astype(F32) + g6.astype(F32)

    grad_q = call(functools.partial(unpack, groups, per), shape((rows, wide), BF16), moved=4 * rows * wide)(back_q)
    return grad_q, total[:block], total[block:]


def solution(mesh):
    ctx, head = mesh.devices.shape
    fine = Mesh(mesh.devices.reshape(ctx // RING, RING, head), ("ring", "z", "head"))
    split = P(("ring", "z", "head"), None)
    return jax.shard_map(
        per_device,
        mesh=fine,
        in_specs=(split, split, split, split, split, split, P(("ring", "z"))),
        out_specs=(split, P(("ring", "z"), "head"), P(("ring", "z"), "head")),
        check_vma=False,
    )
```

```python
import functools
import math

import jax
import jax.numpy as jnp
from jax import lax
from jax.experimental import pallas as pl
from jax.experimental.pallas import tpu as pltpu
from jax.sharding import Mesh
from jax.sharding import PartitionSpec as P

REACH = 6
HD = 128
RING = 8
AUX = 16
CHOOSE_FLOPS = 70_000_000_000
LOG2E = math.log2(math.e)
F32 = jnp.float32
BF16 = jnp.bfloat16
VMEM_LIMIT = 16 * 1024 * 1024
PACK_LIMIT = 60 * 1024 * 1024
LAST = (((1,), (1,)), ((), ()))


def call(kernel, outs, scratch=(), flops=0, moved=0, limit=VMEM_LIMIT, **specs):
    return pl.pallas_call(
        kernel,
        out_shape=outs,
        scratch_shapes=scratch,
        compiler_params=pltpu.CompilerParams(vmem_limit_bytes=limit),
        cost_estimate=pl.CostEstimate(flops=flops, bytes_accessed=moved, transcendentals=0),
        **specs,
    )


def pack_keys(groups, key_hbm, value_hbm, out_ref, k_ref, v_ref, sems):
    rows = k_ref.shape[0]
    fetch(((key_hbm, k_ref), (value_hbm, v_ref)), sems)
    for g in range(groups):
        cols = slice(g * HD, (g + 1) * HD)
        out_ref[g, :rows, :] = k_ref[:, cols]
        out_ref[g, rows:, :] = v_ref[:, cols]


def three_parts(x):
    first = x.astype(BF16)
    rest = x - first.astype(F32)
    second = rest.astype(BF16)
    third = (rest - second.astype(F32)).astype(BF16)
    return first, second, third


def lane_sums(x):
    ones = jnp.ones((8, HD), BF16)
    return sum(lax.dot_general(ones, part, LAST, preferred_element_type=F32) for part in three_parts(x))


def fetch(pairs, sems):
    copies = []
    for n, (source, target) in enumerate(pairs):
        half = source.shape[0] // 2
        for k in range(2):
            rows = slice(k * half, (k + 1) * half)
            copies.append(pltpu.make_async_copy(source.at[rows], target.at[rows], sems.at[n, k]))
    for copy in copies:
        copy.start()
    for copy in copies:
        copy.wait()


def pack_queries(groups, per, query_hbm, dout_hbm, output_hbm, lse_hbm, out_ref, q_ref, d_ref, o_ref, l_ref, sems):
    rows = q_ref.shape[0]
    span = per * rows
    fetch(((query_hbm, q_ref), (dout_hbm, d_ref), (output_hbm, o_ref), (lse_hbm, l_ref)), sems)
    lse = jnp.concatenate([l_ref[...] * LOG2E, jnp.zeros((rows, HD - groups * per), F32)], axis=1)
    lane = lax.broadcasted_iota(jnp.int32, (rows, HD), 1)
    for g in range(groups):
        products, picked = [], []
        for h in range(per):
            cols = slice((g * per + h) * HD, (g * per + h + 1) * HD)
            dout = d_ref[:, cols]
            out_ref[g, h * rows : (h + 1) * rows, :] = q_ref[:, cols]
            out_ref[g, span + h * rows : span + (h + 1) * rows, :] = dout
            products.append(dout.astype(F32) * o_ref[:, cols].astype(F32))
            picked.append(jnp.where(lane == g * per + h, lse, 0.0))
        pieces = []
        for sums in (lane_sums(jnp.concatenate(picked, 0)), lane_sums(jnp.concatenate(products, 0))):
            line = sums[:1]
            high = line.astype(BF16).astype(F32)
            for part in (high, line - high):
                pieces += [part[:, k * HD : (k + 1) * HD] for k in range(span // HD)]
        pieces.append(jnp.zeros((AUX - len(pieces), HD), F32))
        out_ref[g, 2 * span :, :] = jnp.concatenate(pieces, 0).astype(BF16)


def attention(scale, chunks, rows, per, blocks, sources, sinks, first, last, low_ref, pos_ref, msg_ref, *refs):
    count = len(blocks)
    operands = 1 + max(n for n, _ in sources)
    kv_refs, refs = refs[:operands], refs[operands:]
    if not first:
        before_ref, refs = refs[0], refs[1:]
    dq_ref, part_refs, refs = refs[0], refs[1 : len(sinks) + 1], refs[len(sinks) + 1 :]
    k_all, v_all, kt_all, dk_ref, dv_ref = refs[:5]
    bufs = (refs[5:9], refs[9:13])
    span = per * rows
    block = chunks * rows
    half = span // HD
    total = count * block
    for n, (operand, slot) in enumerate(sources):
        at = slice(n * block, (n + 1) * block)
        kv = kv_refs[operand][slot * 2 * block : (slot + 1) * 2 * block].reshape(chunks, 2, rows, HD)
        key = kv[:, 0].reshape(block, HD)
        k_all[at] = key
        v_all[at] = kv[:, 1].reshape(block, HD)
        kt_all[:, at] = key.T
    dk_ref[...] = jnp.zeros_like(dk_ref)
    dv_ref[...] = jnp.zeros_like(dv_ref)

    def window_of(j):
        begin = j * rows if blocks[0] == REACH else 0
        end = total - block + (j + 1) * rows if blocks[-1] == 0 else total
        return begin, end

    def scores(j, sc, gp):
        begin, end = window_of(j)
        sc[: end - begin] = lax.dot_general(k_all[begin:end], msg_ref[j, :span, :], LAST, preferred_element_type=F32)
        gp[: end - begin] = lax.dot_general(
            v_all[begin:end], msg_ref[j, span : 2 * span, :], LAST, preferred_element_type=F32
        )

    def middle(j, sc, gp, pb, ds):
        aux = msg_ref[j, 2 * span :, :].astype(F32)

        def line(at):
            return jnp.concatenate([aux[at + k : at + k + 1] + aux[at + half + k : at + half + k + 1] for k in range(half)], 1)

        lse, delta = line(0), line(2 * half)
        low, pos = low_ref[j : j + 1, :], pos_ref[j : j + 1, :]
        begin, end = window_of(j)
        old_begin, old_end = window_of(j - 2) if j >= 2 else (0, total)
        for a, b in ((old_begin, begin), (end, old_end)):
            if a < b:
                ds[a:b] = jnp.zeros((b - a, span), BF16)
        for n in range(count):
            start, stop = max(begin, n * block), min(end, (n + 1) * block)
            if start >= stop:
                continue
            size = stop - start
            at = slice(start - begin, stop - begin)
            kpos = lax.broadcasted_iota(jnp.int32, (size, span), 0) + (start - n * block - blocks[n] * block)
            allowed = kpos >= low
            if blocks[n] == 0:
                allowed = allowed & (kpos <= pos)
            prob = jnp.where(allowed, jnp.exp2(sc[at] * (scale * LOG2E) - lse), 0.0)
            pb[at] = prob.astype(BF16)
            ds[start:stop] = (prob * (gp[at] - delta)).astype(BF16)

    def sums(j, pb, ds):
        begin, end = window_of(j)
        dv_ref[begin:end] += jnp.dot(pb[: end - begin], msg_ref[j, span : 2 * span, :], preferred_element_type=F32)
        dk_ref[begin:end] += jnp.dot(ds[begin:end], msg_ref[j, :span, :], preferred_element_type=F32)
        dqt = jnp.dot(kt_all[...], ds[...], preferred_element_type=F32)
        cols = slice(j * span, (j + 1) * span)
        if not first:
            dqt = dqt + before_ref[:, cols]
        if last:
            dq_ref[j] = (dqt * scale).T.astype(BF16)
        else:
            dq_ref[:, cols] = dqt

    scores(0, *bufs[0][:2])
    for j in range(chunks):
        sc, gp, pb, ds = bufs[j % 2]
        if j + 1 < chunks:
            scores(j + 1, *bufs[(j + 1) % 2][:2])
        middle(j, sc, gp, pb, ds)
        sums(j, pb, ds)
    for ref, held in zip(part_refs, sinks):
        for slot, s in enumerate(held):
            n = blocks.index(s)
            at = slice(n * block, (n + 1) * block)
            row = slot * 2 * block
            ref[row : row + block] = (dk_ref[at] * scale).astype(ref.dtype)
            ref[row + block : row + 2 * block] = dv_ref[at].astype(ref.dtype)


def attend(scale, chunks, rows, per, low, pos, got, blocks, kv, sources, sinks, before=None, last=False):
    shape = jax.ShapeDtypeStruct
    vmem = pl.BlockSpec(memory_space=pltpu.VMEM)
    span, block = per * rows, chunks * rows
    total = len(blocks) * block
    buffers = [
        pltpu.VMEM((total, span), F32),
        pltpu.VMEM((total, span), F32),
        pltpu.VMEM((total, span), BF16),
        pltpu.VMEM((total, span), BF16),
    ]
    dq = shape((chunks, span, HD), BF16) if last else shape((HD, chunks * span), F32)
    operands = [low, pos, got, *kv] + ([] if before is None else [before])
    return call(
        functools.partial(
            attention, scale, chunks, rows, per, blocks, sources, [held for _, held in sinks], before is None, last
        ),
        [dq] + [shape((len(held) * 2 * block, HD), kind) for kind, held in sinks],
        scratch=[
            pltpu.VMEM((total, HD), BF16),
            pltpu.VMEM((total, HD), BF16),
            pltpu.VMEM((HD, total), BF16),
            pltpu.VMEM((total, HD), F32),
            pltpu.VMEM((total, HD), F32),
            *buffers,
            *buffers,
        ],
        flops=10 * total * chunks * span * HD,
        moved=4 * 1024 * 1024,
        in_specs=[vmem] * len(operands),
        out_specs=[vmem] * (1 + len(sinks)),
    )(*operands)


def choose(reach, z_ref, own_ref, older_ref, *out_refs):
    for s, ref in zip(reach, out_refs):
        ref[...] = jnp.where(z_ref[0] + s < RING, own_ref[...], older_ref[...])


def join(last_ref, next_ref, five_ref, two_ref, five_out, two_out):
    size = five_ref.shape[0]
    for ref, out, part in ((five_ref, five_out, slice(size, 2 * size)), (two_ref, two_out, slice(0, size))):
        out[...] = (ref[...] + last_ref[part].astype(F32) + next_ref[part].astype(F32)).astype(BF16)


def finish(groups, per, got_ref, own_ref, near_ref, far_ref, q_out, k_out, v_out, q_ref, k_ref, v_ref, sems):
    rows, block = q_ref.shape[0], k_ref.shape[0]
    copies = []
    for n, (ref, out, at) in enumerate(((k_ref, k_out, 0), (v_ref, v_out, block))):
        part = slice(at, at + block)
        ref[...] = own_ref[part] + near_ref[part].astype(F32) + far_ref[part].astype(F32)
        copies.append(pltpu.make_async_copy(ref, out, sems.at[n]))
        copies[-1].start()
    for g in range(groups):
        for h in range(per):
            q_ref[:, (g * per + h) * HD : (g * per + h + 1) * HD] = got_ref[g, h * rows : (h + 1) * rows, :]
    half = rows // 2
    for n in range(2):
        part = slice(n * half, (n + 1) * half)
        copies.append(pltpu.make_async_copy(q_ref.at[part], q_out.at[part], sems.at[2 + n]))
        copies[-1].start()
    for copy in copies:
        copy.wait()


def turn(array, axis, by):
    size = lax.axis_size(axis)
    return lax.ppermute(array, axis, [(i, (i + by) % size) for i in range(size)])


def hop(array, by):
    axes = ("ring", "z")
    size = lax.axis_size(axes)
    return lax.ppermute(array, axes, [(i, (i + by) % size) for i in range(size)])


def exchange(array):
    groups, rows, cols = array.shape
    flat = array.reshape(groups * rows, cols)
    return lax.all_to_all(flat, "head", split_axis=0, concat_axis=0, tiled=True).reshape(array.shape)


def per_device(queries, grad_out, outputs, keys, values, log_sum_exp, doc_start):
    rows, wide = queries.shape
    heads = log_sum_exp.shape[1]
    groups = keys.shape[1] // HD
    per = heads // groups
    span = per * rows
    block = doc_start.shape[0]
    chunks = block // rows
    scale = HD ** (-0.5)
    shape = jax.ShapeDtypeStruct
    hbm = pl.BlockSpec(memory_space=pltpu.HBM)
    vmem = pl.BlockSpec(memory_space=pltpu.VMEM)

    kv_own = call(
        functools.partial(pack_keys, groups),
        shape((groups, 2 * rows, HD), BF16),
        scratch=[pltpu.VMEM((rows, groups * HD), BF16)] * 2 + [pltpu.SemaphoreType.DMA((2, 2))],
        moved=4 * rows * groups * HD * 2,
        in_specs=[hbm] * 2,
        out_specs=vmem,
        limit=PACK_LIMIT,
    )(keys, values)
    kv_own = exchange(kv_own)
    message = call(
        functools.partial(pack_queries, groups, per),
        shape((groups, 2 * span + AUX, HD), BF16),
        scratch=[pltpu.VMEM((rows, wide), BF16)] * 3
        + [pltpu.VMEM((rows, heads), F32), pltpu.SemaphoreType.DMA((4, 2))],
        moved=5 * rows * wide * 2,
        in_specs=[hbm] * 4,
        out_specs=vmem,
        limit=PACK_LIMIT,
    )(queries, grad_out, outputs, log_sum_exp)
    message, kv_own = lax.optimization_barrier((message, kv_own))
    kv_own = kv_own.reshape(2 * block, HD)
    kv_older = turn(kv_own, "ring", 1)
    kv = {}
    got = exchange(message)
    z = lax.axis_index("z")

    reach = (6, 4, 3, 1, 5, 2)
    sent = call(
        functools.partial(choose, reach),
        [shape((2 * block, HD), BF16)] * REACH,
        flops=CHOOSE_FLOPS,
        in_specs=[pl.BlockSpec(memory_space=pltpu.SMEM), vmem, vmem],
        out_specs=[vmem] * REACH,
    )(z.reshape(1), kv_own, kv_older)
    kv = {s: turn(array, "z", s) for s, array in zip(reach, sent)}
    kv[0] = kv_own

    first = (lax.axis_index("ring") * RING + z) * block
    low = jnp.tile((doc_start - first).reshape(chunks, 1, rows), (1, per, 1)).reshape(chunks, span)
    pos = jnp.tile(jnp.arange(block, dtype=jnp.int32).reshape(chunks, 1, rows), (1, per, 1)).reshape(chunks, span)

    run = functools.partial(attend, scale, chunks, rows, per, low, pos, got)

    dq, g14, g36 = run(
        (6, 4, 3, 1), [kv[s] for s in (6, 4, 3, 1)], [(n, 0) for n in range(4)], [(BF16, (1, 4)), (BF16, (3, 6))]
    )
    from_last, from_next = hop(g14, 1), hop(g36, -1)
    dq, g5, g2, g0 = run(
        (5, 2, 0),
        [kv[s] for s in (5, 2, 0)],
        [(n, 0) for n in range(3)],
        [(F32, (5,)), (F32, (2,)), (F32, (0,))],
        before=dq,
        last=True,
    )
    back_q = exchange(dq)
    size = 2 * block
    g5, g2 = call(
        join, [shape((size, HD), BF16)] * 2, flops=CHOOSE_FLOPS, in_specs=[vmem] * 4, out_specs=[vmem] * 2
    )(from_last, from_next, g5, g2)
    g5, g2 = hop(g5, -5), hop(g2, -2)

    grad_q, grad_k, grad_v = call(
        functools.partial(finish, groups, per),
        [shape((rows, wide), BF16), shape((block, HD), F32), shape((block, HD), F32)],
        scratch=[
            pltpu.VMEM((rows, wide), BF16),
            pltpu.VMEM((block, HD), F32),
            pltpu.VMEM((block, HD), F32),
            pltpu.SemaphoreType.DMA((4,)),
        ],
        moved=4 * rows * wide,
        in_specs=[vmem] * 4,
        out_specs=[hbm] * 3,
    )(back_q, g0, g2, g5)
    return grad_q, grad_k, grad_v


def solution(mesh):
    ctx, head = mesh.devices.shape
    fine = Mesh(mesh.devices.reshape(ctx // RING, RING, head), ("ring", "z", "head"))
    split = P(("ring", "z", "head"), None)
    return jax.shard_map(
        per_device,
        mesh=fine,
        in_specs=(split, split, split, split, split, split, P(("ring", "z"))),
        out_specs=(split, P(("ring", "z"), "head"), P(("ring", "z"), "head")),
        check_vma=False,
    )
```

```python
import functools
import math

import jax
import jax.numpy as jnp
from jax import lax
from jax.experimental import pallas as pl
from jax.experimental.pallas import tpu as pltpu
from jax.sharding import Mesh
from jax.sharding import PartitionSpec as P

REACH = 6
HD = 128
RING = 8
AUX = 16
CHOOSE_FLOPS = 70_000_000_000
LOG2E = math.log2(math.e)
F32 = jnp.float32
BF16 = jnp.bfloat16
VMEM_LIMIT = 16 * 1024 * 1024
PACK_LIMIT = 60 * 1024 * 1024
LAST = (((1,), (1,)), ((), ()))


def call(kernel, outs, scratch=(), flops=0, moved=0, limit=VMEM_LIMIT, **specs):
    return pl.pallas_call(
        kernel,
        out_shape=outs,
        scratch_shapes=scratch,
        compiler_params=pltpu.CompilerParams(vmem_limit_bytes=limit),
        cost_estimate=pl.CostEstimate(flops=flops, bytes_accessed=moved, transcendentals=0),
        **specs,
    )


def pack_keys(groups, key_hbm, value_hbm, out_ref, k_ref, v_ref, sems):
    rows = k_ref.shape[0]
    fetch(((key_hbm, k_ref), (value_hbm, v_ref)), sems)
    for g in range(groups):
        cols = slice(g * HD, (g + 1) * HD)
        out_ref[g, :rows, :] = k_ref[:, cols]
        out_ref[g, rows:, :] = v_ref[:, cols]


def three_parts(x):
    first = x.astype(BF16)
    rest = x - first.astype(F32)
    second = rest.astype(BF16)
    third = (rest - second.astype(F32)).astype(BF16)
    return first, second, third


def lane_sums(x):
    ones = jnp.ones((8, HD), BF16)
    return sum(lax.dot_general(ones, part, LAST, preferred_element_type=F32) for part in three_parts(x))


def fetch(pairs, sems):
    copies = []
    for n, (source, target) in enumerate(pairs):
        half = source.shape[0] // 2
        for k in range(2):
            rows = slice(k * half, (k + 1) * half)
            copies.append(pltpu.make_async_copy(source.at[rows], target.at[rows], sems.at[n, k]))
    for copy in copies:
        copy.start()
    for copy in copies:
        copy.wait()


def pack_queries(groups, per, query_hbm, dout_hbm, output_hbm, lse_hbm, out_ref, q_ref, d_ref, o_ref, l_ref, sems):
    rows = q_ref.shape[0]
    span = per * rows
    fetch(((query_hbm, q_ref), (dout_hbm, d_ref), (output_hbm, o_ref), (lse_hbm, l_ref)), sems)
    lse = jnp.concatenate([l_ref[...] * LOG2E, jnp.zeros((rows, HD - groups * per), F32)], axis=1)
    lane = lax.broadcasted_iota(jnp.int32, (rows, HD), 1)
    for g in range(groups):
        products, picked = [], []
        for h in range(per):
            cols = slice((g * per + h) * HD, (g * per + h + 1) * HD)
            dout = d_ref[:, cols]
            out_ref[g, h * rows : (h + 1) * rows, :] = q_ref[:, cols]
            out_ref[g, span + h * rows : span + (h + 1) * rows, :] = dout
            products.append(dout.astype(F32) * o_ref[:, cols].astype(F32))
            picked.append(jnp.where(lane == g * per + h, lse, 0.0))
        pieces = []
        for sums in (lane_sums(jnp.concatenate(picked, 0)), lane_sums(jnp.concatenate(products, 0))):
            line = sums[:1]
            high = line.astype(BF16).astype(F32)
            for part in (high, line - high):
                pieces += [part[:, k * HD : (k + 1) * HD] for k in range(span // HD)]
        pieces.append(jnp.zeros((AUX - len(pieces), HD), F32))
        out_ref[g, 2 * span :, :] = jnp.concatenate(pieces, 0).astype(BF16)


def attention(scale, chunks, rows, per, blocks, sources, sinks, first, last, low_ref, pos_ref, msg_ref, *refs):
    count = len(blocks)
    operands = 1 + max(n for n, _ in sources)
    kv_refs, refs = refs[:operands], refs[operands:]
    if not first:
        before_ref, refs = refs[0], refs[1:]
    dq_ref, part_refs, refs = refs[0], refs[1 : len(sinks) + 1], refs[len(sinks) + 1 :]
    k_all, v_all, kt_all, dk_ref, dv_ref = refs[:5]
    bufs = (refs[5:9], refs[9:13])
    span = per * rows
    block = chunks * rows
    half = span // HD
    total = count * block
    for n, (operand, slot) in enumerate(sources):
        at = slice(n * block, (n + 1) * block)
        kv = kv_refs[operand][slot * 2 * block : (slot + 1) * 2 * block].reshape(chunks, 2, rows, HD)
        key = kv[:, 0].reshape(block, HD)
        k_all[at] = key
        v_all[at] = kv[:, 1].reshape(block, HD)
        kt_all[:, at] = key.T
    dk_ref[...] = jnp.zeros_like(dk_ref)
    dv_ref[...] = jnp.zeros_like(dv_ref)

    def window_of(j):
        begin = j * rows if blocks[0] == REACH else 0
        end = total - block + (j + 1) * rows if blocks[-1] == 0 else total
        return begin, end

    def scores(j, sc, gp):
        begin, end = window_of(j)
        sc[: end - begin] = lax.dot_general(k_all[begin:end], msg_ref[j, :span, :], LAST, preferred_element_type=F32)
        gp[: end - begin] = lax.dot_general(
            v_all[begin:end], msg_ref[j, span : 2 * span, :], LAST, preferred_element_type=F32
        )

    def middle(j, sc, gp, pb, ds):
        aux = msg_ref[j, 2 * span :, :].astype(F32)

        def line(at):
            return jnp.concatenate([aux[at + k : at + k + 1] + aux[at + half + k : at + half + k + 1] for k in range(half)], 1)

        lse, delta = line(0), line(2 * half)
        low, pos = low_ref[j : j + 1, :], pos_ref[j : j + 1, :]
        begin, end = window_of(j)
        old_begin, old_end = window_of(j - 2) if j >= 2 else (0, total)
        for a, b in ((old_begin, begin), (end, old_end)):
            if a < b:
                ds[a:b] = jnp.zeros((b - a, span), BF16)
        for n in range(count):
            start, stop = max(begin, n * block), min(end, (n + 1) * block)
            if start >= stop:
                continue
            size = stop - start
            at = slice(start - begin, stop - begin)
            kpos = lax.broadcasted_iota(jnp.int32, (size, span), 0) + (start - n * block - blocks[n] * block)
            allowed = kpos >= low
            if blocks[n] == 0:
                allowed = allowed & (kpos <= pos)
            prob = jnp.where(allowed, jnp.exp2(sc[at] * (scale * LOG2E) - lse), 0.0)
            pb[at] = prob.astype(BF16)
            ds[start:stop] = (prob * (gp[at] - delta)).astype(BF16)

    def sums(j, pb, ds):
        begin, end = window_of(j)
        dv_ref[begin:end] += jnp.dot(pb[: end - begin], msg_ref[j, span : 2 * span, :], preferred_element_type=F32)
        dk_ref[begin:end] += jnp.dot(ds[begin:end], msg_ref[j, :span, :], preferred_element_type=F32)
        dqt = jnp.dot(kt_all[...], ds[...], preferred_element_type=F32)
        cols = slice(j * span, (j + 1) * span)
        if not first:
            dqt = dqt + before_ref[:, cols]
        if last:
            dq_ref[j] = (dqt * scale).astype(BF16).T
        else:
            dq_ref[:, cols] = dqt

    scores(0, *bufs[0][:2])
    for j in range(chunks):
        sc, gp, pb, ds = bufs[j % 2]
        if j + 1 < chunks:
            scores(j + 1, *bufs[(j + 1) % 2][:2])
        middle(j, sc, gp, pb, ds)
        sums(j, pb, ds)
    for ref, held in zip(part_refs, sinks):
        for slot, s in enumerate(held):
            n = blocks.index(s)
            at = slice(n * block, (n + 1) * block)
            row = slot * 2 * block
            ref[row : row + block] = (dk_ref[at] * scale).astype(ref.dtype)
            ref[row + block : row + 2 * block] = dv_ref[at].astype(ref.dtype)


def attend(scale, chunks, rows, per, low, pos, got, blocks, kv, sources, sinks, before=None, last=False):
    shape = jax.ShapeDtypeStruct
    vmem = pl.BlockSpec(memory_space=pltpu.VMEM)
    span, block = per * rows, chunks * rows
    total = len(blocks) * block
    buffers = [
        pltpu.VMEM((total, span), F32),
        pltpu.VMEM((total, span), F32),
        pltpu.VMEM((total, span), BF16),
        pltpu.VMEM((total, span), BF16),
    ]
    dq = shape((chunks, span, HD), BF16) if last else shape((HD, chunks * span), F32)
    operands = [low, pos, got, *kv] + ([] if before is None else [before])
    return call(
        functools.partial(
            attention, scale, chunks, rows, per, blocks, sources, [held for _, held in sinks], before is None, last
        ),
        [dq] + [shape((len(held) * 2 * block, HD), kind) for kind, held in sinks],
        scratch=[
            pltpu.VMEM((total, HD), BF16),
            pltpu.VMEM((total, HD), BF16),
            pltpu.VMEM((HD, total), BF16),
            pltpu.VMEM((total, HD), F32),
            pltpu.VMEM((total, HD), F32),
            *buffers,
            *buffers,
        ],
        flops=10 * total * chunks * span * HD,
        moved=4 * 1024 * 1024,
        in_specs=[vmem] * len(operands),
        out_specs=[vmem] * (1 + len(sinks)),
    )(*operands)


def choose(reach, z_ref, own_ref, older_ref, *out_refs):
    for s, ref in zip(reach, out_refs):
        ref[...] = jnp.where(z_ref[0] + s < RING, own_ref[...], older_ref[...])


def join(last_ref, next_ref, five_ref, two_ref, five_out, two_out):
    size = five_ref.shape[0]
    for ref, out, part in ((five_ref, five_out, slice(size, 2 * size)), (two_ref, two_out, slice(0, size))):
        out[...] = (ref[...] + last_ref[part].astype(F32) + next_ref[part].astype(F32)).astype(BF16)


def finish(groups, per, got_ref, own_ref, far_ref, near_ref, q_out, k_out, v_out, q_ref, k_ref, v_ref, sems):
    rows, block = q_ref.shape[0], k_ref.shape[0]
    copies = []
    for n, (ref, out, at) in enumerate(((k_ref, k_out, 0), (v_ref, v_out, block))):
        part = slice(at, at + block)
        ref[...] = own_ref[part] + near_ref[part].astype(F32) + far_ref[part].astype(F32)
        copies.append(pltpu.make_async_copy(ref, out, sems.at[n]))
        copies[-1].start()
    for g in range(groups):
        for h in range(per):
            q_ref[:, (g * per + h) * HD : (g * per + h + 1) * HD] = got_ref[g, h * rows : (h + 1) * rows, :]
    half = rows // 2
    for n in range(2):
        part = slice(n * half, (n + 1) * half)
        copies.append(pltpu.make_async_copy(q_ref.at[part], q_out.at[part], sems.at[2 + n]))
        copies[-1].start()
    for copy in copies:
        copy.wait()


def turn(array, axis, by):
    size = lax.axis_size(axis)
    return lax.ppermute(array, axis, [(i, (i + by) % size) for i in range(size)])


def hop(array, by):
    axes = ("ring", "z")
    size = lax.axis_size(axes)
    return lax.ppermute(array, axes, [(i, (i + by) % size) for i in range(size)])


def exchange(array):
    groups, rows, cols = array.shape
    flat = array.reshape(groups * rows, cols)
    return lax.all_to_all(flat, "head", split_axis=0, concat_axis=0, tiled=True).reshape(array.shape)


def per_device(queries, grad_out, outputs, keys, values, log_sum_exp, doc_start):
    rows, wide = queries.shape
    heads = log_sum_exp.shape[1]
    groups = keys.shape[1] // HD
    per = heads // groups
    span = per * rows
    block = doc_start.shape[0]
    chunks = block // rows
    scale = HD ** (-0.5)
    shape = jax.ShapeDtypeStruct
    hbm = pl.BlockSpec(memory_space=pltpu.HBM)
    vmem = pl.BlockSpec(memory_space=pltpu.VMEM)

    kv_own = call(
        functools.partial(pack_keys, groups),
        shape((groups, 2 * rows, HD), BF16),
        scratch=[pltpu.VMEM((rows, groups * HD), BF16)] * 2 + [pltpu.SemaphoreType.DMA((2, 2))],
        moved=4 * rows * groups * HD * 2,
        in_specs=[hbm] * 2,
        out_specs=vmem,
        limit=PACK_LIMIT,
    )(keys, values)
    kv_own = exchange(kv_own)
    message = call(
        functools.partial(pack_queries, groups, per),
        shape((groups, 2 * span + AUX, HD), BF16),
        scratch=[pltpu.VMEM((rows, wide), BF16)] * 3
        + [pltpu.VMEM((rows, heads), F32), pltpu.SemaphoreType.DMA((4, 2))],
        moved=5 * rows * wide * 2,
        in_specs=[hbm] * 4,
        out_specs=vmem,
        limit=PACK_LIMIT,
    )(queries, grad_out, outputs, log_sum_exp)
    message, kv_own = lax.optimization_barrier((message, kv_own))
    kv_own = kv_own.reshape(2 * block, HD)
    kv_older = turn(kv_own, "ring", 1)
    kv = {}
    got = exchange(message)
    z = lax.axis_index("z")

    reach = (4, 3, 6, 1, 5, 2)
    sent = call(
        functools.partial(choose, reach),
        [shape((2 * block, HD), BF16)] * REACH,
        flops=CHOOSE_FLOPS,
        in_specs=[pl.BlockSpec(memory_space=pltpu.SMEM), vmem, vmem],
        out_specs=[vmem] * REACH,
    )(z.reshape(1), kv_own, kv_older)
    kv = {s: turn(array, "z", s) for s, array in zip(reach, sent)}
    kv[0] = kv_own

    first = (lax.axis_index("ring") * RING + z) * block
    low = jnp.tile((doc_start - first).reshape(chunks, 1, rows), (1, per, 1)).reshape(chunks, span)
    pos = jnp.tile(jnp.arange(block, dtype=jnp.int32).reshape(chunks, 1, rows), (1, per, 1)).reshape(chunks, span)

    run = functools.partial(attend, scale, chunks, rows, per, low, pos, got)

    dq, g14, g36 = run(
        (6, 4, 3, 1), [kv[s] for s in (4, 3, 6, 1)], [(2, 0), (0, 0), (1, 0), (3, 0)], [(BF16, (1, 4)), (BF16, (3, 6))]
    )
    from_last, from_next = hop(g14, 1), hop(g36, -1)
    dq, g5, g2, g0 = run(
        (5, 2, 0),
        [kv[s] for s in (5, 2, 0)],
        [(n, 0) for n in range(3)],
        [(F32, (5,)), (F32, (2,)), (F32, (0,))],
        before=dq,
        last=True,
    )
    back_q = exchange(dq)
    size = 2 * block
    g5, g2 = call(
        join, [shape((size, HD), BF16)] * 2, flops=CHOOSE_FLOPS, in_specs=[vmem] * 4, out_specs=[vmem] * 2
    )(from_last, from_next, g5, g2)
    g5, g2 = hop(g5, -5), hop(g2, -2)

    grad_q, grad_k, grad_v = call(
        functools.partial(finish, groups, per),
        [shape((rows, wide), BF16), shape((block, HD), F32), shape((block, HD), F32)],
        scratch=[
            pltpu.VMEM((rows, wide), BF16),
            pltpu.VMEM((block, HD), F32),
            pltpu.VMEM((block, HD), F32),
            pltpu.SemaphoreType.DMA((4,)),
        ],
        moved=4 * rows * wide,
        in_specs=[vmem] * 4,
        out_specs=[hbm] * 3,
    )(back_q, g0, g5, g2)
    return grad_q, grad_k, grad_v


def solution(mesh):
    ctx, head = mesh.devices.shape
    fine = Mesh(mesh.devices.reshape(ctx // RING, RING, head), ("ring", "z", "head"))
    split = P(("ring", "z", "head"), None)
    return jax.shard_map(
        per_device,
        mesh=fine,
        in_specs=(split, split, split, split, split, split, P(("ring", "z"))),
        out_specs=(split, P(("ring", "z"), "head"), P(("ring", "z"), "head")),
        check_vma=False,
    )
```

```python
import functools
import math

import jax
import jax.numpy as jnp
from jax import lax
from jax.experimental import pallas as pl
from jax.experimental.pallas import tpu as pltpu
from jax.sharding import Mesh
from jax.sharding import PartitionSpec as P

REACH = 6
HD = 128
RING = 8
AUX = 16
CHOOSE_FLOPS = 70_000_000_000
LOG2E = math.log2(math.e)
F32 = jnp.float32
BF16 = jnp.bfloat16
VMEM_LIMIT = 16 * 1024 * 1024
PACK_LIMIT = 60 * 1024 * 1024
LAST = (((1,), (1,)), ((), ()))


def call(kernel, outs, scratch=(), flops=0, moved=0, limit=VMEM_LIMIT, **specs):
    return pl.pallas_call(
        kernel,
        out_shape=outs,
        scratch_shapes=scratch,
        compiler_params=pltpu.CompilerParams(vmem_limit_bytes=limit),
        cost_estimate=pl.CostEstimate(flops=flops, bytes_accessed=moved, transcendentals=0),
        **specs,
    )


def pack_keys(groups, key_hbm, value_hbm, out_ref, k_ref, v_ref, sems):
    rows = k_ref.shape[0]
    fetch(((key_hbm, k_ref), (value_hbm, v_ref)), sems)
    for g in range(groups):
        cols = slice(g * HD, (g + 1) * HD)
        out_ref[g, :rows, :] = k_ref[:, cols]
        out_ref[g, rows:, :] = v_ref[:, cols]


def three_parts(x):
    first = x.astype(BF16)
    rest = x - first.astype(F32)
    second = rest.astype(BF16)
    third = (rest - second.astype(F32)).astype(BF16)
    return first, second, third


def lane_sums(x):
    ones = jnp.ones((8, HD), BF16)
    return sum(lax.dot_general(ones, part, LAST, preferred_element_type=F32) for part in three_parts(x))


def fetch(pairs, sems):
    copies = []
    for n, (source, target) in enumerate(pairs):
        half = source.shape[0] // 2
        for k in range(2):
            rows = slice(k * half, (k + 1) * half)
            copies.append(pltpu.make_async_copy(source.at[rows], target.at[rows], sems.at[n, k]))
    for copy in copies:
        copy.start()
    for copy in copies:
        copy.wait()


def pack_queries(groups, per, query_hbm, dout_hbm, output_hbm, lse_hbm, out_ref, q_ref, d_ref, o_ref, l_ref, sems):
    rows = q_ref.shape[0]
    span = per * rows
    fetch(((query_hbm, q_ref), (dout_hbm, d_ref), (output_hbm, o_ref), (lse_hbm, l_ref)), sems)
    lse = jnp.concatenate([l_ref[...] * LOG2E, jnp.zeros((rows, HD - groups * per), F32)], axis=1)
    lane = lax.broadcasted_iota(jnp.int32, (rows, HD), 1)
    for g in range(groups):
        products, picked = [], []
        for h in range(per):
            cols = slice((g * per + h) * HD, (g * per + h + 1) * HD)
            dout = d_ref[:, cols]
            out_ref[g, h * rows : (h + 1) * rows, :] = q_ref[:, cols]
            out_ref[g, span + h * rows : span + (h + 1) * rows, :] = dout
            products.append(dout.astype(F32) * o_ref[:, cols].astype(F32))
            picked.append(jnp.where(lane == g * per + h, lse, 0.0))
        pieces = []
        for sums in (lane_sums(jnp.concatenate(picked, 0)), lane_sums(jnp.concatenate(products, 0))):
            line = sums[:1]
            high = line.astype(BF16).astype(F32)
            for part in (high, line - high):
                pieces += [part[:, k * HD : (k + 1) * HD] for k in range(span // HD)]
        pieces.append(jnp.zeros((AUX - len(pieces), HD), F32))
        out_ref[g, 2 * span :, :] = jnp.concatenate(pieces, 0).astype(BF16)


def attention(scale, chunks, rows, per, blocks, sources, sinks, first, last, low_ref, pos_ref, msg_ref, *refs):
    count = len(blocks)
    operands = 1 + max(n for n, _ in sources)
    kv_refs, refs = refs[:operands], refs[operands:]
    if not first:
        before_ref, refs = refs[0], refs[1:]
    dq_ref, part_refs, refs = refs[0], refs[1 : len(sinks) + 1], refs[len(sinks) + 1 :]
    k_all, v_all, kt_all, dk_ref, dv_ref = refs[:5]
    bufs = (refs[5:9], refs[9:13])
    span = per * rows
    block = chunks * rows
    half = span // HD
    total = count * block
    for n, (operand, slot) in enumerate(sources):
        at = slice(n * block, (n + 1) * block)
        kv = kv_refs[operand][slot * 2 * block : (slot + 1) * 2 * block].reshape(chunks, 2, rows, HD)
        key = kv[:, 0].reshape(block, HD)
        k_all[at] = key
        v_all[at] = kv[:, 1].reshape(block, HD)
        kt_all[:, at] = key.T
    dk_ref[...] = jnp.zeros_like(dk_ref)
    dv_ref[...] = jnp.zeros_like(dv_ref)

    def window_of(j):
        begin = j * rows if blocks[0] == REACH else 0
        end = total - block + (j + 1) * rows if blocks[-1] == 0 else total
        return begin, end

    def scores(j, sc, gp):
        begin, end = window_of(j)
        sc[: end - begin] = lax.dot_general(k_all[begin:end], msg_ref[j, :span, :], LAST, preferred_element_type=F32)
        gp[: end - begin] = lax.dot_general(
            v_all[begin:end], msg_ref[j, span : 2 * span, :], LAST, preferred_element_type=F32
        )

    def middle(j, sc, gp, pb, ds):
        aux = msg_ref[j, 2 * span :, :].astype(F32)

        def line(at):
            return jnp.concatenate([aux[at + k : at + k + 1] + aux[at + half + k : at + half + k + 1] for k in range(half)], 1)

        lse, delta = line(0), line(2 * half)
        low, pos = low_ref[j : j + 1, :], pos_ref[j : j + 1, :]
        begin, end = window_of(j)
        old_begin, old_end = window_of(j - 2) if j >= 2 else (0, total)
        for a, b in ((old_begin, begin), (end, old_end)):
            if a < b:
                ds[a:b] = jnp.zeros((b - a, span), BF16)
        for n in range(count):
            start, stop = max(begin, n * block), min(end, (n + 1) * block)
            if start >= stop:
                continue
            size = stop - start
            at = slice(start - begin, stop - begin)
            kpos = lax.broadcasted_iota(jnp.int32, (size, span), 0) + (start - n * block - blocks[n] * block)
            allowed = kpos >= low
            if blocks[n] == 0:
                allowed = allowed & (kpos <= pos)
            prob = jnp.where(allowed, jnp.exp2(sc[at] * (scale * LOG2E) - lse), 0.0)
            pb[at] = prob.astype(BF16)
            ds[start:stop] = (prob * (gp[at] - delta)).astype(BF16)

    def sums(j, pb, ds):
        begin, end = window_of(j)
        dv_ref[begin:end] += jnp.dot(pb[: end - begin], msg_ref[j, span : 2 * span, :], preferred_element_type=F32)
        dk_ref[begin:end] += jnp.dot(ds[begin:end], msg_ref[j, :span, :], preferred_element_type=F32)
        dqt = jnp.dot(kt_all[...], ds[...], preferred_element_type=F32)
        cols = slice(j * span, (j + 1) * span)
        if not first:
            dqt = dqt + before_ref[:, cols]
        if last:
            dq_ref[j] = (dqt * scale).astype(BF16).T
        else:
            dq_ref[:, cols] = dqt

    scores(0, *bufs[0][:2])
    for j in range(chunks):
        sc, gp, pb, ds = bufs[j % 2]
        if j + 1 < chunks:
            scores(j + 1, *bufs[(j + 1) % 2][:2])
        middle(j, sc, gp, pb, ds)
        sums(j, pb, ds)
    for ref, held in zip(part_refs, sinks):
        for slot, s in enumerate(held):
            n = blocks.index(s)
            at = slice(n * block, (n + 1) * block)
            row = slot * 2 * block
            ref[row : row + block] = (dk_ref[at] * scale).astype(ref.dtype)
            ref[row + block : row + 2 * block] = dv_ref[at].astype(ref.dtype)


def attend(scale, chunks, rows, per, low, pos, got, blocks, kv, sources, sinks, before=None, last=False):
    shape = jax.ShapeDtypeStruct
    vmem = pl.BlockSpec(memory_space=pltpu.VMEM)
    span, block = per * rows, chunks * rows
    total = len(blocks) * block
    buffers = [
        pltpu.VMEM((total, span), F32),
        pltpu.VMEM((total, span), F32),
        pltpu.VMEM((total, span), BF16),
        pltpu.VMEM((total, span), BF16),
    ]
    dq = shape((chunks, span, HD), BF16) if last else shape((HD, chunks * span), F32)
    operands = [low, pos, got, *kv] + ([] if before is None else [before])
    return call(
        functools.partial(
            attention, scale, chunks, rows, per, blocks, sources, [held for _, held in sinks], before is None, last
        ),
        [dq] + [shape((len(held) * 2 * block, HD), kind) for kind, held in sinks],
        scratch=[
            pltpu.VMEM((total, HD), BF16),
            pltpu.VMEM((total, HD), BF16),
            pltpu.VMEM((HD, total), BF16),
            pltpu.VMEM((total, HD), F32),
            pltpu.VMEM((total, HD), F32),
            *buffers,
            *buffers,
        ],
        flops=10 * total * chunks * span * HD,
        moved=4 * 1024 * 1024,
        in_specs=[vmem] * len(operands),
        out_specs=[vmem] * (1 + len(sinks)),
    )(*operands)


def choose(reach, z_ref, own_ref, older_ref, *out_refs):
    for s, ref in zip(reach, out_refs):
        ref[...] = jnp.where(z_ref[0] + s < RING, own_ref[...], older_ref[...])


def join(last_ref, next_ref, five_ref, two_ref, five_out, two_out):
    size = five_ref.shape[0]
    for ref, out, part in ((five_ref, five_out, slice(size, 2 * size)), (two_ref, two_out, slice(0, size))):
        out[...] = (ref[...] + last_ref[part].astype(F32) + next_ref[part].astype(F32)).astype(BF16)


def finish(own_ref, far_ref, near_ref, k_out, v_out):
    block = k_out.shape[0]
    for n, out in enumerate((k_out, v_out)):
        part = slice(n * block, (n + 1) * block)
        out[...] = own_ref[part] + far_ref[part].astype(F32) + near_ref[part].astype(F32)


def unpack(groups, per, got_ref, out_ref):
    rows = out_ref.shape[0]
    for g in range(groups):
        for h in range(per):
            out_ref[:, (g * per + h) * HD : (g * per + h + 1) * HD] = got_ref[g, h * rows : (h + 1) * rows, :]


def turn(array, axis, by):
    size = lax.axis_size(axis)
    return lax.ppermute(array, axis, [(i, (i + by) % size) for i in range(size)])


def hop(array, by):
    axes = ("ring", "z")
    size = lax.axis_size(axes)
    return lax.ppermute(array, axes, [(i, (i + by) % size) for i in range(size)])


def exchange(array):
    groups, rows, cols = array.shape
    flat = array.reshape(groups * rows, cols)
    return lax.all_to_all(flat, "head", split_axis=0, concat_axis=0, tiled=True).reshape(array.shape)


def per_device(queries, grad_out, outputs, keys, values, log_sum_exp, doc_start):
    rows, wide = queries.shape
    heads = log_sum_exp.shape[1]
    groups = keys.shape[1] // HD
    per = heads // groups
    span = per * rows
    block = doc_start.shape[0]
    chunks = block // rows
    scale = HD ** (-0.5)
    shape = jax.ShapeDtypeStruct
    hbm = pl.BlockSpec(memory_space=pltpu.HBM)
    vmem = pl.BlockSpec(memory_space=pltpu.VMEM)

    kv_own = call(
        functools.partial(pack_keys, groups),
        shape((groups, 2 * rows, HD), BF16),
        scratch=[pltpu.VMEM((rows, groups * HD), BF16)] * 2 + [pltpu.SemaphoreType.DMA((2, 2))],
        moved=4 * rows * groups * HD * 2,
        in_specs=[hbm] * 2,
        out_specs=vmem,
        limit=PACK_LIMIT,
    )(keys, values)
    kv_own = exchange(kv_own)
    message = call(
        functools.partial(pack_queries, groups, per),
        shape((groups, 2 * span + AUX, HD), BF16),
        scratch=[pltpu.VMEM((rows, wide), BF16)] * 3
        + [pltpu.VMEM((rows, heads), F32), pltpu.SemaphoreType.DMA((4, 2))],
        moved=5 * rows * wide * 2,
        in_specs=[hbm] * 4,
        out_specs=vmem,
        limit=PACK_LIMIT,
    )(queries, grad_out, outputs, log_sum_exp)
    message, kv_own = lax.optimization_barrier((message, kv_own))
    kv_own = kv_own.reshape(2 * block, HD)
    kv_older = turn(kv_own, "ring", 1)
    kv = {}
    got = exchange(message)
    z = lax.axis_index("z")

    reach = (4, 3, 6, 1, 5, 2)
    sent = call(
        functools.partial(choose, reach),
        [shape((2 * block, HD), BF16)] * REACH,
        flops=CHOOSE_FLOPS,
        in_specs=[pl.BlockSpec(memory_space=pltpu.SMEM), vmem, vmem],
        out_specs=[vmem] * REACH,
    )(z.reshape(1), kv_own, kv_older)
    kv = {s: turn(array, "z", s) for s, array in zip(reach, sent)}
    kv[0] = kv_own

    first = (lax.axis_index("ring") * RING + z) * block
    low = jnp.tile((doc_start - first).reshape(chunks, 1, rows), (1, per, 1)).reshape(chunks, span)
    pos = jnp.tile(jnp.arange(block, dtype=jnp.int32).reshape(chunks, 1, rows), (1, per, 1)).reshape(chunks, span)

    run = functools.partial(attend, scale, chunks, rows, per, low, pos, got)

    dq, g14, g36 = run(
        (6, 4, 3, 1), [kv[s] for s in (4, 3, 6, 1)], [(2, 0), (0, 0), (1, 0), (3, 0)], [(BF16, (1, 4)), (BF16, (3, 6))]
    )
    from_last, from_next = hop(g14, 1), hop(g36, -1)
    dq, g5, g2, g0 = run(
        (5, 2, 0),
        [kv[s] for s in (5, 2, 0)],
        [(n, 0) for n in range(3)],
        [(F32, (5,)), (F32, (2,)), (F32, (0,))],
        before=dq,
        last=True,
    )
    back_q = exchange(dq)
    size = 2 * block
    g5, g2 = call(
        join, [shape((size, HD), BF16)] * 2, flops=CHOOSE_FLOPS, in_specs=[vmem] * 4, out_specs=[vmem] * 2
    )(from_last, from_next, g5, g2)
    g5, g2 = hop(g5, -5), hop(g2, -2)

    grad_q = call(
        functools.partial(unpack, groups, per),
        shape((rows, wide), BF16),
        flops=CHOOSE_FLOPS,
        in_specs=[vmem],
        out_specs=vmem,
    )(back_q)
    grad_k, grad_v = call(
        finish,
        [shape((block, HD), F32)] * 2,
        in_specs=[vmem] * 3,
        out_specs=[vmem] * 2,
    )(g0, g5, g2)
    return grad_q, grad_k, grad_v


def solution(mesh):
    ctx, head = mesh.devices.shape
    fine = Mesh(mesh.devices.reshape(ctx // RING, RING, head), ("ring", "z", "head"))
    split = P(("ring", "z", "head"), None)
    return jax.shard_map(
        per_device,
        mesh=fine,
        in_specs=(split, split, split, split, split, split, P(("ring", "z"))),
        out_specs=(split, P(("ring", "z"), "head"), P(("ring", "z"), "head")),
        check_vma=False,
    )
```
